32 devices in a mesh: dp: 2 (over x), fsdp: 16 (over z, y, core).
Axes of the slice: x: 2, y: 2, z: 4, core: 2. Of those that a mesh axis runs over, the one named last changes fastest.
Arguments:
- context: bfloat16 [2048, 8192], P(('dp', 'fsdp')), may hold values from -18 to 18
- residual: bfloat16 [2048, 8192], P('dp', 'fsdp'), may hold values from -45 to 45
- out_weight: bfloat16 [8192, 8192], P(None, 'fsdp'), may hold values from -0.0625 to 0.0625
- norm_gain: float32 [8192], P('fsdp'), may hold values from 0.5 to 1.5
- exit_layer: int32 [16], replicated, may hold values from 0 to 79, as said below
- destination: int32 [16], replicated, may hold values from 0 to 1, as said below
Outputs:
- hidden: bfloat16 [2048, 8192], P('dp', 'fsdp')
- normed: bfloat16 [2048, 8192], P('dp', 'fsdp')
The draws below stay inside these ranges and needn't reach their ends.
Inputs may be any that keep to these rules, and one draw needn't show every extreme that they name: `destination`: at each position within the data groups, the destinations of the 2 passages at that position are all different. `exit_layer`: at each position i within the data groups, the passage of group i % 2 at that position is living.
All inputs are finite; a program needn't handle non-finite values.
Results may differ from the reference program's by a relative error of at most 0.0051.
Values may be sent and summed in bfloat16 or wider, within the bound.
A program may use at most 128 MiB of HBM per device.

```python
import jax
import jax.numpy as jnp
from jax import lax

D = 8192
LAYERS = 80
LAYER = 32
PLEN = 128
P_GRP = 8
TOKENS = 2048
CTXW = 8192
N_DP = 2


def row_scales(key):
    return 0.3 * 10.0 ** jax.random.uniform(jax.random.fold_in(key, 11), (TOKENS, 1), jnp.float32)


def draw_context(key, part):
    scales = row_scales(key)
    key = jax.random.fold_in(key, 1)
    values = jnp.clip(jax.random.normal(key, (TOKENS, CTXW), jnp.float32), -6.0, 6.0)
    return (values * scales).astype(jnp.bfloat16)


def draw_residual(key, part):
    scales = row_scales(key)
    key = jax.random.fold_in(key, 2)
    columns = jnp.arange(D, dtype=jnp.float32) / D
    values = jnp.clip(jax.random.normal(key, (TOKENS, D), jnp.float32), -6.0, 6.0)
    column_scale = 10.0 ** columns
    return (0.25 * values * scales * column_scale[None, :]).astype(jnp.bfloat16)


def draw_destination(key, part):
    key = jax.random.fold_in(key, 3)
    subkeys = jax.random.split(key, P_GRP)
    orders = jax.vmap(lambda single: jax.random.permutation(single, N_DP))(subkeys)
    return jnp.transpose(orders).reshape(N_DP * P_GRP).astype(jnp.int32)


def draw_exit_layer(key, part):
    key = jax.random.fold_in(key, 4)
    coin_key, late_key, early_key = jax.random.split(key, 3)
    coins = jax.random.randint(coin_key, (N_DP, P_GRP), 0, 2)
    groups = jnp.arange(N_DP, dtype=jnp.int32)[:, None]
    positions = jnp.arange(P_GRP, dtype=jnp.int32)[None, :]
    forced = positions % N_DP == groups
    alive = (coins == 1) | forced
    late = jax.random.randint(late_key, (N_DP, P_GRP), LAYER + 1, LAYERS)
    early = jax.random.randint(early_key, (N_DP, P_GRP), 0, LAYER + 1)
    return jnp.where(alive, late, early).reshape(N_DP * P_GRP).astype(jnp.int32)


def level_of(key, extent, pieces, smallest, largest):
    def one(dim, parts):
        draws = jax.random.uniform(jax.random.fold_in(jax.random.fold_in(key, 6), dim), (parts,), jnp.float32, smallest / len(pieces), largest / len(pieces))
        return jnp.repeat(jnp.exp(draws), extent[dim] // parts).reshape((-1,) + (1,) * (len(extent) - dim - 1))

    factor_of = one(*pieces[0])
    for cut in pieces[1:]:
        factor_of = factor_of * one(*cut)
    return factor_of


def normal_values(own_key, dims, width, limit, cuts=(), kind=jnp.bfloat16):
    entries = width * jax.random.normal(own_key, dims, jnp.float32)
    if cuts:
        entries = entries * level_of(own_key, dims, cuts, -0.22, 0.18)
    return jnp.clip(entries, -limit, limit).astype(kind)


def setup_inputs(seed: int = 0) -> dict:
    splits = jax.random.split(jax.random.key(seed), 7)
    context = draw_context(jax.random.fold_in(splits[6], 71), 0)
    residual = draw_residual(jax.random.fold_in(splits[6], 71), 0)
    out_weight = normal_values(splits[2], (CTXW, D), CTXW ** -0.5, 0.0625, ((1, 16),))
    norm_gain = jnp.clip(1.0 + 0.1 * jax.random.normal(splits[3], (D,), jnp.float32), 0.5, 1.5)
    exit_layer = draw_exit_layer(jax.random.fold_in(splits[6], 71), 0)
    destination = draw_destination(jax.random.fold_in(splits[6], 71), 0)
    return dict(context=context, residual=residual, out_weight=out_weight, norm_gain=norm_gain, exit_layer=exit_layer, destination=destination)


def reference(context, residual, out_weight, norm_gain, exit_layer, destination):
    projected = jnp.dot(context.astype(jnp.float32), out_weight.astype(jnp.float32), precision=lax.Precision.HIGHEST)
    stream = (projected + residual.astype(jnp.float32)).astype(jnp.bfloat16)
    stream_wide = lax.optimization_barrier(stream).astype(jnp.float32)
    living = exit_layer > LAYER
    dest_table = destination.reshape(N_DP, P_GRP)
    live_table = living.reshape(N_DP, P_GRP)
    targets = jnp.arange(N_DP, dtype=jnp.int32)
    routing = ((dest_table[:, None, :] == targets[None, :, None]) & live_table[:, None, :]).astype(jnp.float32)
    blocks = stream_wide.reshape(N_DP, P_GRP, PLEN, D)
    moved = jnp.einsum('sdi,sitc->ditc', routing, blocks).reshape(N_DP * P_GRP * PLEN, D)
    hidden = moved.astype(jnp.bfloat16)
    hidden_wide = lax.optimization_barrier(hidden).astype(jnp.float32)
    mean_sq = lax.optimization_barrier(jnp.mean(hidden_wide * hidden_wide, axis=1, keepdims=True))
    normed = (hidden_wide * lax.rsqrt(mean_sq + 1e-05) * norm_gain.astype(jnp.float32)[None, :]).astype(jnp.bfloat16)
    return (hidden, normed)
```

```python
import functools

import jax
import jax.numpy as jnp
from jax import lax
from jax.experimental import pallas as pl
from jax.experimental.pallas import tpu as pltpu
from jax.sharding import PartitionSpec as P

D = 8192
LAYER = 32
PLEN = 128
LANES = 128
MESH = pl.DeviceIdType.MESH


def kernel(
    groups, members, pieces,
    context_ref, residual_ref, weight_ref, gain_ref, exit_ref, dest_ref,
    hidden_ref, normed_ref,
    ctx, weight, residual, acc, stream, incoming, hidden, normed, squares,
    ring_send, ring_recv, core_send, core_recv, own_sem, weight_sem, residual_sem,
    peer_send, peer_recv, square_send, square_recv, hidden_sem, normed_sem,
):
    rows, depth = context_ref.shape
    width = depth // pieces
    passages = residual_ref.shape[0] // PLEN
    chips = members // 2
    group = lax.axis_index("dp")
    me = lax.axis_index("fsdp")
    core = lax.rem(me, 2)
    chip = me // 2

    def chip_at(place):
        return jnp.where(place < chips // 2, 2 * place, 2 * (chips - 1 - place) + 1)

    place = jnp.where(lax.rem(chip, 2) == 0, chip // 2, chips - 1 - chip // 2)
    ahead = lax.rem(place + jnp.where(core == 0, 1, chips - 1), chips)
    target = chip_at(ahead) * 2 + core
    sibling = chip * 2 + 1 - core

    def shard_of(step, half):
        shift = chips - step if half == 0 else step
        return chip_at(lax.rem(place + shift, chips)) * 2 + half

    def ring_copy(step, piece, source=None):
        return pltpu.make_async_remote_copy(
            src_ref=ctx.at[step, piece, core] if source is None else source,
            dst_ref=ctx.at[step + 1, piece, core],
            send_sem=ring_send.at[step, piece],
            recv_sem=ring_recv.at[step + 1, piece],
            device_id=(group, target),
            device_id_type=MESH,
        )

    def core_copy(step, piece, source=None):
        return pltpu.make_async_remote_copy(
            src_ref=ctx.at[step, piece, core] if source is None else source,
            dst_ref=ctx.at[step, piece, core],
            send_sem=core_send.at[step, piece],
            recv_sem=core_recv.at[step, piece],
            device_id=(group, sibling),
            device_id_type=MESH,
        )

    def own_piece(piece):
        return context_ref.at[:, pl.ds(piece * width, width)]

    def own_copy(piece):
        return pltpu.make_async_copy(own_piece(piece), ctx.at[0, piece, core], own_sem.at[piece])

    def weight_copy(piece):
        return pltpu.make_async_copy(
            weight_ref.at[pl.ds(piece * width, width), :], weight.at[piece], weight_sem.at[piece]
        )

    residual_copy = pltpu.make_async_copy(residual_ref, residual, residual_sem)

    def peer_copy(step, distance):
        return pltpu.make_async_remote_copy(
            src_ref=stream.at[step],
            dst_ref=incoming.at[distance - 1, step],
            send_sem=peer_send.at[distance - 1, step],
            recv_sem=peer_recv.at[distance - 1, step],
            device_id=(lax.rem(group + distance, groups), me),
            device_id_type=MESH,
        )

    def square_copy(distance):
        return pltpu.make_async_remote_copy(
            src_ref=squares.at[0],
            dst_ref=squares.at[distance],
            send_sem=square_send.at[distance],
            recv_sem=square_recv.at[distance],
            device_id=(group, lax.rem(me + distance, members)),
            device_id_type=MESH,
        )

    def rows_of(shard):
        return pl.ds(pl.multiple_of(shard * rows, rows), rows)

    def hidden_copy(step, half):
        where = rows_of(shard_of(step, half))
        return pltpu.make_async_copy(
            hidden.at[where, :], hidden_ref.at[where, :], hidden_sem.at[step, half]
        )

    def normed_copy(shard):
        where = pl.ds(shard * rows, rows)
        return pltpu.make_async_copy(
            normed.at[where, :], normed_ref.at[where, :], normed_sem.at[shard]
        )

    for piece in range(pieces):
        own_copy(piece).start()
    for piece in range(pieces):
        weight_copy(piece).start()
    residual_copy.start()

    barrier = pltpu.get_barrier_semaphore()

    def greet(distance, carry):
        pl.semaphore_signal(
            barrier, inc=1, device_id=(group, lax.rem(me + distance, members)), device_id_type=MESH
        )
        return carry

    lax.fori_loop(1, members, greet, 0)
    for distance in range(1, groups):
        pl.semaphore_signal(
            barrier, inc=1, device_id=(lax.rem(group + distance, groups), me), device_id_type=MESH
        )
    pl.semaphore_wait(barrier, members - 1 + groups - 1)

    for piece in range(pieces):
        ring_copy(0, piece, own_piece(piece)).start()
        core_copy(0, piece, own_piece(piece)).start()

    def finish(step):
        for distance in range(1, groups):
            peer_copy(step, distance).wait_recv()
        total = jnp.zeros((2 * rows, LANES), jnp.float32)
        halves = []
        for half in range(2):
            shard = shard_of(step, half)
            position = shard * rows // PLEN
            chosen = None
            for distance in range(groups):
                source = lax.rem(group + groups - distance, groups)
                where = source * passages + position
                taken = jnp.logical_and(exit_ref[where] > LAYER, dest_ref[where] == group)
                block = stream[step, half] if distance == 0 else incoming[distance - 1, step, half]
                term = block.astype(jnp.float32) * taken.astype(jnp.int32).astype(jnp.float32)
                chosen = term if chosen is None else chosen + term
            hidden[rows_of(shard), :] = chosen.astype(hidden.dtype)
            hidden_copy(step, half).start()
            square = chosen * chosen
            parts = [square[:, at : at + LANES] for at in range(0, square.shape[1], LANES)]
            halves.append(functools.reduce(jnp.add, parts))
        if 2 * rows < LANES:
            halves.append(jnp.zeros((LANES - 2 * rows, LANES), jnp.float32))
        total = jnp.concatenate(halves, axis=0)
        sums = jnp.sum(total.T, axis=0, keepdims=True)
        for half in range(2):
            squares[0, pl.ds(shard_of(step, half), 1), :] = sums

    def body(turn, carry):
        @pl.when(jnp.logical_and(turn >= pieces, turn < chips * pieces))
        def _():
            step, piece = turn // pieces, lax.rem(turn, pieces)
            ring_copy(step - 1, piece).wait_recv()

            @pl.when(step < chips - 1)
            def _():
                ring_copy(step, piece).start()

            core_copy(step, piece).start()

        @pl.when(turn >= 1)
        def _():
            step, piece = (turn - 1) // pieces, lax.rem(turn - 1, pieces)

            @pl.when(step == 0)
            def _():
                own_copy(piece).wait()
                weight_copy(piece).wait()

            core_copy(step, piece).wait_recv()
            product = jnp.dot(
                ctx[step, piece].reshape(2 * rows, width),
                weight[piece],
                preferred_element_type=jnp.float32,
            )

            @pl.when(piece == 0)
            def _():
                acc[...] = product

            @pl.when(piece > 0)
            def _():
                acc[...] += product

            @pl.when(piece == pieces - 1)
            def _():
                @pl.when(step == 0)
                def _():
                    residual_copy.wait()

                for half in range(2):
                    before = residual[rows_of(shard_of(step, half)), :].astype(jnp.float32)
                    stream[step, half] = (acc[half * rows : (half + 1) * rows, :] + before).astype(
                        stream.dtype
                    )
                for distance in range(1, groups):
                    peer_copy(step, distance).start()

                @pl.when(step > 0)
                def _():
                    finish(step - 1)

        return carry

    lax.fori_loop(0, chips * pieces + 1, body, 0)
    finish(chips - 1)

    def send_squares(distance, carry):
        square_copy(distance).start()
        return carry

    def take_squares(distance, carry):
        square_copy(distance).wait_recv()
        return carry

    lax.fori_loop(1, members, send_squares, 0)
    lax.fori_loop(1, members, take_squares, 0)
    total = jnp.sum(squares[...], axis=0)
    if members < LANES:
        total = jnp.concatenate(
            [total, jnp.zeros((LANES - members, LANES), jnp.float32)], axis=0
        )
    inverse_rms = lax.rsqrt(total / D + 1e-05).T
    gain = gain_ref[...]
    for shard in range(members):
        half = shard % 2
        scale = inverse_rms[half * rows : (half + 1) * rows, shard : shard + 1]
        where = slice(shard * rows, (shard + 1) * rows)
        normed[where, :] = (hidden[where, :].astype(jnp.float32) * scale * gain).astype(normed.dtype)
        normed_copy(shard).start()

    def drain(turn, carry):
        step, piece = turn // pieces, lax.rem(turn, pieces)

        @pl.when(step < chips - 1)
        def _():
            ring_copy(step, piece).wait_send()

        core_copy(step, piece).wait_send()
        return carry

    lax.fori_loop(0, chips * pieces, drain, 0)

    def drain_steps(step, carry):
        for distance in range(1, groups):
            peer_copy(step, distance).wait_send()
        for half in range(2):
            hidden_copy(step, half).wait()
        return carry

    lax.fori_loop(0, chips, drain_steps, 0)

    def drain_squares(distance, carry):
        square_copy(distance).wait_send()
        return carry

    lax.fori_loop(1, members, drain_squares, 0)
    for shard in range(members):
        normed_copy(shard).wait()


def local(groups, members, context, residual, out_weight, norm_gain, exit_layer, destination):
    rows, depth = context.shape
    group_rows, columns = residual.shape
    chips = members // 2
    pieces = max(1, min(4, rows // 16))
    anywhere = pl.BlockSpec(memory_space=pl.ANY)
    scalars = pl.BlockSpec(memory_space=pltpu.SMEM)
    out = jax.ShapeDtypeStruct((group_rows, columns), jnp.bfloat16)
    dma = pltpu.SemaphoreType.DMA
    return pl.pallas_call(
        functools.partial(kernel, groups, members, pieces),
        out_shape=(out, out),
        in_specs=[anywhere, anywhere, anywhere, pl.BlockSpec(memory_space=pltpu.VMEM), scalars, scalars],
        out_specs=(anywhere, anywhere),
        scratch_shapes=[
            pltpu.VMEM((chips, pieces, 2, rows, depth // pieces), jnp.bfloat16),
            pltpu.VMEM((pieces, depth // pieces, columns), jnp.bfloat16),
            pltpu.VMEM((group_rows, columns), jnp.bfloat16),
            pltpu.VMEM((2 * rows, columns), jnp.float32),
            pltpu.VMEM((chips, 2, rows, columns), jnp.bfloat16),
            pltpu.VMEM((groups - 1, chips, 2, rows, columns), jnp.bfloat16),
            pltpu.VMEM((group_rows, columns), jnp.bfloat16),
            pltpu.VMEM((group_rows, columns), jnp.bfloat16),
            pltpu.VMEM((members, members, LANES), jnp.float32),
            dma((chips, pieces)),
            dma((chips, pieces)),
            dma((chips, pieces)),
            dma((chips, pieces)),
            dma((pieces,)),
            dma((pieces,)),
            dma(()),
            dma((groups - 1, chips)),
            dma((groups - 1, chips)),
            dma((members,)),
            dma((members,)),
            dma((chips, 2)),
            dma((members,)),
        ],
        compiler_params=pltpu.CompilerParams(
            collective_id=0, has_side_effects=True, vmem_limit_bytes=52 * 1024 * 1024
        ),
        cost_estimate=pl.CostEstimate(
            flops=2 * group_rows * depth * columns,
            bytes_accessed=2 * (rows * depth + depth * columns + 3 * group_rows * columns),
            transcendentals=0,
        ),
    )(context, residual, out_weight, norm_gain.reshape(1, columns), exit_layer, destination)


def solution(mesh):
    in_specs = (P(("dp", "fsdp"), None), P("dp", "fsdp"), P(None, "fsdp"), P("fsdp"), P(), P())
    out_specs = (P("dp", "fsdp"), P("dp", "fsdp"))
    body = functools.partial(local, mesh.shape["dp"], mesh.shape["fsdp"])
    return jax.shard_map(body, mesh=mesh, in_specs=in_specs, out_specs=out_specs, check_vma=False)
```

```python
import functools

import jax
import jax.numpy as jnp
from jax import lax
from jax.experimental import pallas as pl
from jax.experimental.pallas import tpu as pltpu
from jax.sharding import PartitionSpec as P

D = 8192
LAYER = 32
PLEN = 128
LANES = 128
MESH = pl.DeviceIdType.MESH


def kernel(
    groups, members, pieces,
    context_ref, residual_ref, weight_ref, gain_ref, exit_ref, dest_ref,
    hidden, normed,
    ctx, weight, residual, acc, stream, incoming, squares,
    ring_send, ring_recv, core_send, core_recv, own_sem, weight_sem, residual_sem,
    peer_send, peer_recv, square_send, square_recv,
):
    rows, depth = context_ref.shape
    width = depth // pieces
    passages = residual_ref.shape[0] // PLEN
    chips = members // 2
    group = lax.axis_index("dp")
    me = lax.axis_index("fsdp")
    core = lax.rem(me, 2)
    chip = me // 2

    def chip_at(place):
        return jnp.where(place < chips // 2, 2 * place, 2 * (chips - 1 - place) + 1)

    place = jnp.where(lax.rem(chip, 2) == 0, chip // 2, chips - 1 - chip // 2)
    ahead = lax.rem(place + jnp.where(core == 0, 1, chips - 1), chips)
    target = chip_at(ahead) * 2 + core
    sibling = chip * 2 + 1 - core

    def shard_of(step, half):
        shift = chips - step if half == 0 else step
        return chip_at(lax.rem(place + shift, chips)) * 2 + half

    def ring_copy(step, piece, source=None):
        return pltpu.make_async_remote_copy(
            src_ref=ctx.at[step, piece, core] if source is None else source,
            dst_ref=ctx.at[step + 1, piece, core],
            send_sem=ring_send.at[step, piece],
            recv_sem=ring_recv.at[step + 1, piece],
            device_id=(group, target),
            device_id_type=MESH,
        )

    def core_copy(step, piece, source=None):
        return pltpu.make_async_remote_copy(
            src_ref=ctx.at[step, piece, core] if source is None else source,
            dst_ref=ctx.at[step, piece, core],
            send_sem=core_send.at[step, piece],
            recv_sem=core_recv.at[step, piece],
            device_id=(group, sibling),
            device_id_type=MESH,
        )

    def own_piece(piece):
        return context_ref.at[:, pl.ds(piece * width, width)]

    def own_copy(piece):
        return pltpu.make_async_copy(own_piece(piece), ctx.at[0, piece, core], own_sem.at[piece])

    def weight_copy(piece):
        return pltpu.make_async_copy(
            weight_ref.at[pl.ds(piece * width, width), :], weight.at[piece], weight_sem.at[piece]
        )

    residual_copy = pltpu.make_async_copy(residual_ref, residual, residual_sem)

    def peer_copy(step, distance):
        return pltpu.make_async_remote_copy(
            src_ref=stream.at[step],
            dst_ref=incoming.at[distance - 1, step],
            send_sem=peer_send.at[distance - 1, step],
            recv_sem=peer_recv.at[distance - 1, step],
            device_id=(lax.rem(group + distance, groups), me),
            device_id_type=MESH,
        )

    def square_copy(distance):
        return pltpu.make_async_remote_copy(
            src_ref=squares.at[0],
            dst_ref=squares.at[distance],
            send_sem=square_send.at[distance],
            recv_sem=square_recv.at[distance],
            device_id=(group, lax.rem(me + distance, members)),
            device_id_type=MESH,
        )

    def rows_of(shard):
        return pl.ds(pl.multiple_of(shard * rows, rows), rows)

    for piece in range(pieces):
        own_copy(piece).start()
    for piece in range(pieces):
        weight_copy(piece).start()
    residual_copy.start()
    squares[0] = jnp.zeros(squares.shape[1:], jnp.float32)

    barrier = pltpu.get_barrier_semaphore()

    behind = lax.rem(place + jnp.where(core == 0, chips - 1, 1), chips)
    for member in (target, chip_at(behind) * 2 + core, sibling):
        pl.semaphore_signal(barrier, inc=1, device_id=(group, member), device_id_type=MESH)
    for distance in range(1, groups):
        pl.semaphore_signal(
            barrier, inc=1, device_id=(lax.rem(group + distance, groups), me), device_id_type=MESH
        )
    pl.semaphore_wait(barrier, 3 + groups - 1)

    for piece in range(pieces):
        ring_copy(0, piece, own_piece(piece)).start()
        core_copy(0, piece, own_piece(piece)).start()

    def finish(step):
        for distance in range(1, groups):
            peer_copy(step, distance).wait_recv()
        halves = []
        for half in range(2):
            shard = shard_of(step, half)
            position = shard * rows // PLEN
            chosen = None
            for distance in range(groups):
                source = lax.rem(group + groups - distance, groups)
                where = source * passages + position
                taken = jnp.logical_and(exit_ref[where] > LAYER, dest_ref[where] == group)
                block = stream[step, half] if distance == 0 else incoming[distance - 1, step, half]
                term = block.astype(jnp.float32) * taken.astype(jnp.int32).astype(jnp.float32)
                chosen = term if chosen is None else chosen + term
            hidden[rows_of(shard), :] = chosen.astype(hidden.dtype)
            square = chosen * chosen
            parts = [square[:, at : at + LANES] for at in range(0, square.shape[1], LANES)]
            halves.append(functools.reduce(jnp.add, parts))
        if 2 * rows < LANES:
            halves.append(jnp.zeros((LANES - 2 * rows, LANES), jnp.float32))
        total = jnp.concatenate(halves, axis=0)
        sums = jnp.sum(total.T, axis=0, keepdims=True)
        lane = lax.broadcasted_iota(jnp.int32, sums.shape, 1)
        for half in range(2):
            own = jnp.logical_and(lane >= half * rows, lane < (half + 1) * rows)
            squares[0, pl.ds(shard_of(step, half) // 2, 1), :] += jnp.where(own, sums, 0.0)

    def body(turn, carry):
        @pl.when(jnp.logical_and(turn >= pieces, turn < chips * pieces))
        def _():
            step, piece = turn // pieces, lax.rem(turn, pieces)
            ring_copy(step - 1, piece).wait_recv()

            @pl.when(step < chips - 1)
            def _():
                ring_copy(step, piece).start()

            core_copy(step, piece).start()

        @pl.when(turn >= 1)
        def _():
            step, piece = (turn - 1) // pieces, lax.rem(turn - 1, pieces)

            @pl.when(step == 0)
            def _():
                own_copy(piece).wait()
                weight_copy(piece).wait()

            core_copy(step, piece).wait_recv()
            product = jnp.dot(
                ctx[step, piece].reshape(2 * rows, width),
                weight[piece],
                preferred_element_type=jnp.float32,
            )

            @pl.when(piece == 0)
            def _():
                acc[...] = product

            @pl.when(piece > 0)
            def _():
                acc[...] += product

            @pl.when(piece == pieces - 1)
            def _():
                @pl.when(step == 0)
                def _():
                    residual_copy.wait()

                for half in range(2):
                    before = residual[rows_of(shard_of(step, half)), :].astype(jnp.float32)
                    stream[step, half] = (acc[half * rows : (half + 1) * rows, :] + before).astype(
                        stream.dtype
                    )
                for distance in range(1, groups):
                    peer_copy(step, distance).start()

                @pl.when(step > 0)
                def _():
                    finish(step - 1)

        return carry

    lax.fori_loop(0, chips * pieces + 1, body, 0)
    finish(chips - 1)

    def send_squares(distance, carry):
        square_copy(distance).start()
        return carry

    def take_squares(distance, carry):
        square_copy(distance).wait_recv()
        return carry

    lax.fori_loop(1, members, send_squares, 0)
    lax.fori_loop(1, members, take_squares, 0)
    total = jnp.sum(squares[...], axis=0)
    if chips < LANES:
        total = jnp.concatenate(
            [total, jnp.zeros((LANES - chips, LANES), jnp.float32)], axis=0
        )
    inverse_rms = lax.rsqrt(total / D + 1e-05).T
    gain = gain_ref[...]
    for shard in range(members):
        half = shard % 2
        scale = inverse_rms[half * rows : (half + 1) * rows, shard // 2 : shard // 2 + 1]
        where = slice(shard * rows, (shard + 1) * rows)
        normed[where, :] = (hidden[where, :].astype(jnp.float32) * scale * gain).astype(normed.dtype)

    def drain(turn, carry):
        step, piece = turn // pieces, lax.rem(turn, pieces)

        @pl.when(step < chips - 1)
        def _():
            ring_copy(step, piece).wait_send()

        core_copy(step, piece).wait_send()
        return carry

    lax.fori_loop(0, chips * pieces, drain, 0)

    def drain_steps(step, carry):
        for distance in range(1, groups):
            peer_copy(step, distance).wait_send()
        return carry

    lax.fori_loop(0, chips, drain_steps, 0)

    def drain_squares(distance, carry):
        square_copy(distance).wait_send()
        return carry

    lax.fori_loop(1, members, drain_squares, 0)


def local(groups, members, context, residual, out_weight, norm_gain, exit_layer, destination):
    rows, depth = context.shape
    group_rows, columns = residual.shape
    chips = members // 2
    pieces = max(1, min(4, rows // 16))
    anywhere = pl.BlockSpec(memory_space=pl.ANY)
    scalars = pl.BlockSpec(memory_space=pltpu.SMEM)
    out = jax.ShapeDtypeStruct((group_rows, columns), jnp.bfloat16)
    dma = pltpu.SemaphoreType.DMA
    return pl.pallas_call(
        functools.partial(kernel, groups, members, pieces),
        out_shape=(out, out),
        in_specs=[anywhere, anywhere, anywhere, pl.BlockSpec(memory_space=pltpu.VMEM), scalars, scalars],
        out_specs=(pl.BlockSpec(memory_space=pltpu.VMEM),) * 2,
        scratch_shapes=[
            pltpu.VMEM((chips, pieces, 2, rows, depth // pieces), jnp.bfloat16),
            pltpu.VMEM((pieces, depth // pieces, columns), jnp.bfloat16),
            pltpu.VMEM((group_rows, columns), jnp.bfloat16),
            pltpu.VMEM((2 * rows, columns), jnp.float32),
            pltpu.VMEM((chips, 2, rows, columns), jnp.bfloat16),
            pltpu.VMEM((groups - 1, chips, 2, rows, columns), jnp.bfloat16),
            pltpu.VMEM((members, chips, LANES), jnp.float32),
            dma((chips, pieces)),
            dma((chips, pieces)),
            dma((chips, pieces)),
            dma((chips, pieces)),
            dma((pieces,)),
            dma((pieces,)),
            dma(()),
            dma((groups - 1, chips)),
            dma((groups - 1, chips)),
            dma((members,)),
            dma((members,)),
        ],
        compiler_params=pltpu.CompilerParams(
            collective_id=0, has_side_effects=True, vmem_limit_bytes=51 * 1024 * 1024
        ),
        cost_estimate=pl.CostEstimate(
            flops=2 * group_rows * depth * columns,
            bytes_accessed=2 * (rows * depth + depth * columns + 3 * group_rows * columns),
            transcendentals=0,
        ),
    )(context, residual, out_weight, norm_gain.reshape(1, columns), exit_layer, destination)


def solution(mesh):
    in_specs = (P(("dp", "fsdp"), None), P("dp", "fsdp"), P(None, "fsdp"), P("fsdp"), P(), P())
    out_specs = (P("dp", "fsdp"), P("dp", "fsdp"))
    body = functools.partial(local, mesh.shape["dp"], mesh.shape["fsdp"])
    return jax.shard_map(body, mesh=mesh, in_specs=in_specs, out_specs=out_specs, check_vma=False)
```

```python
import functools

import jax
import jax.numpy as jnp
from jax import lax
from jax.experimental import pallas as pl
from jax.experimental.pallas import tpu as pltpu
from jax.sharding import PartitionSpec as P

D = 8192
LAYER = 32
PLEN = 128
LANES = 128
MESH = pl.DeviceIdType.MESH


def kernel(
    groups, members, pieces,
    context_ref, residual_ref, weight_ref, gain_ref, exit_ref, dest_ref,
    hidden, normed,
    ctx, weight, residual, acc, stream, incoming, squares,
    ring_send, ring_recv, core_send, core_recv, own_sem, weight_sem, residual_sem,
    peer_send, peer_recv, square_send, square_recv,
):
    rows, depth = context_ref.shape
    width = depth // pieces
    passages = residual_ref.shape[0] // PLEN
    chips = members // 2
    group = lax.axis_index("dp")
    me = lax.axis_index("fsdp")
    core = lax.rem(me, 2)
    chip = me // 2

    def chip_at(place):
        return jnp.where(place < chips // 2, 2 * place, 2 * (chips - 1 - place) + 1)

    place = jnp.where(lax.rem(chip, 2) == 0, chip // 2, chips - 1 - chip // 2)
    ahead = lax.rem(place + jnp.where(core == 0, 1, chips - 1), chips)
    target = chip_at(ahead) * 2 + core
    sibling = chip * 2 + 1 - core

    def shard_of(step, half):
        shift = chips - step if half == 0 else step
        return chip_at(lax.rem(place + shift, chips)) * 2 + half

    def ring_copy(step, piece, source=None):
        return pltpu.make_async_remote_copy(
            src_ref=ctx.at[step, piece, core] if source is None else source,
            dst_ref=ctx.at[step + 1, piece, core],
            send_sem=ring_send.at[step, piece],
            recv_sem=ring_recv.at[step + 1, piece],
            device_id=(group, target),
            device_id_type=MESH,
        )

    def core_copy(step, piece, source=None):
        return pltpu.make_async_remote_copy(
            src_ref=ctx.at[step, piece, core] if source is None else source,
            dst_ref=ctx.at[step, piece, core],
            send_sem=core_send.at[step, piece],
            recv_sem=core_recv.at[step, piece],
            device_id=(group, sibling),
            device_id_type=MESH,
        )

    def own_piece(piece):
        return context_ref.at[:, pl.ds(piece * width, width)]

    def own_copy(piece):
        return pltpu.make_async_copy(own_piece(piece), ctx.at[0, piece, core], own_sem.at[piece])

    def weight_copy(piece):
        return pltpu.make_async_copy(
            weight_ref.at[pl.ds(piece * width, width), :], weight.at[piece], weight_sem.at[piece]
        )

    residual_copy = pltpu.make_async_copy(residual_ref, residual, residual_sem)

    def peer_copy(step, distance):
        return pltpu.make_async_remote_copy(
            src_ref=stream.at[step],
            dst_ref=incoming.at[distance - 1, step],
            send_sem=peer_send.at[distance - 1, step],
            recv_sem=peer_recv.at[distance - 1, step],
            device_id=(lax.rem(group + distance, groups), me),
            device_id_type=MESH,
        )

    def square_copy(index):
        return pltpu.make_async_remote_copy(
            src_ref=squares.at[0],
            dst_ref=squares.at[index],
            send_sem=square_send.at[index],
            recv_sem=square_recv.at[index],
            device_id=(
                lax.rem(group + index // members, groups),
                lax.rem(me + lax.rem(index, members), members),
            ),
            device_id_type=MESH,
        )

    def taken_of(shard, distance):
        where = lax.rem(group + groups - distance, groups) * passages + shard * rows // PLEN
        taken = jnp.logical_and(exit_ref[where] > LAYER, dest_ref[where] == group)
        return taken.astype(jnp.int32).astype(jnp.float32)

    def rows_of(shard):
        return pl.ds(pl.multiple_of(shard * rows, rows), rows)

    for piece in range(pieces):
        own_copy(piece).start()
    for piece in range(pieces):
        weight_copy(piece).start()
    residual_copy.start()
    squares[0] = jnp.zeros(squares.shape[1:], jnp.float32)

    barrier = pltpu.get_barrier_semaphore()

    behind = lax.rem(place + jnp.where(core == 0, chips - 1, 1), chips)
    for member in (target, chip_at(behind) * 2 + core, sibling):
        pl.semaphore_signal(barrier, inc=1, device_id=(group, member), device_id_type=MESH)
    for distance in range(1, groups):
        pl.semaphore_signal(
            barrier, inc=1, device_id=(lax.rem(group + distance, groups), me), device_id_type=MESH
        )
    pl.semaphore_wait(barrier, 3 + groups - 1)

    for piece in range(pieces):
        ring_copy(0, piece, own_piece(piece)).start()
        core_copy(0, piece, own_piece(piece)).start()

    def add_squares(step, blocks):
        halves = []
        for block in blocks:
            square = block * block
            parts = [square[:, at : at + LANES] for at in range(0, square.shape[1], LANES)]
            halves.append(functools.reduce(jnp.add, parts))
        if 2 * rows < LANES:
            halves.append(jnp.zeros((LANES - 2 * rows, LANES), jnp.float32))
        sums = jnp.sum(jnp.concatenate(halves, axis=0).T, axis=0, keepdims=True)
        lane = lax.broadcasted_iota(jnp.int32, sums.shape, 1)
        for half in range(2):
            own = jnp.logical_and(lane >= half * rows, lane < (half + 1) * rows)
            squares[0, pl.ds(shard_of(step, half) // 2, 1), :] += jnp.where(own, sums, 0.0)

    def finish(step):
        for distance in range(1, groups):
            peer_copy(step, distance).wait_recv()
        for half in range(2):
            shard = shard_of(step, half)
            chosen = None
            for distance in range(groups):
                block = stream[step, half] if distance == 0 else incoming[distance - 1, step, half]
                term = block.astype(jnp.float32) * taken_of(shard, distance)
                chosen = term if chosen is None else chosen + term
            hidden[rows_of(shard), :] = chosen.astype(hidden.dtype)

    def body(turn, carry):
        @pl.when(jnp.logical_and(turn >= pieces, turn < chips * pieces))
        def _():
            step, piece = turn // pieces, lax.rem(turn, pieces)
            ring_copy(step - 1, piece).wait_recv()

            @pl.when(step < chips - 1)
            def _():
                ring_copy(step, piece).start()

            core_copy(step, piece).start()

        @pl.when(turn >= 1)
        def _():
            step, piece = (turn - 1) // pieces, lax.rem(turn - 1, pieces)

            @pl.when(step == 0)
            def _():
                own_copy(piece).wait()
                weight_copy(piece).wait()

            core_copy(step, piece).wait_recv()
            product = jnp.dot(
                ctx[step, piece].reshape(2 * rows, width),
                weight[piece],
                preferred_element_type=jnp.float32,
            )

            @pl.when(piece == 0)
            def _():
                acc[...] = product

            @pl.when(piece > 0)
            def _():
                acc[...] += product

            @pl.when(piece == pieces - 1)
            def _():
                @pl.when(step == 0)
                def _():
                    residual_copy.wait()

                blocks = []
                for half in range(2):
                    before = residual[rows_of(shard_of(step, half)), :].astype(jnp.float32)
                    block = (acc[half * rows : (half + 1) * rows, :] + before).astype(stream.dtype)
                    stream[step, half] = block
                    blocks.append(block.astype(jnp.float32))
                for distance in range(1, groups):
                    peer_copy(step, distance).start()

                add_squares(step, blocks)

                @pl.when(jnp.logical_and(step > 0, step < chips - 1))
                def _():
                    finish(step - 1)

        return carry

    lax.fori_loop(0, chips * pieces + 1, body, 0)

    def send_squares(index, carry):
        square_copy(index).start()
        return carry

    def take_squares(index, carry):
        square_copy(index).wait_recv()
        return carry

    lax.fori_loop(1, groups * members, send_squares, 0)
    finish(chips - 2)
    finish(chips - 1)
    lax.fori_loop(1, groups * members, take_squares, 0)
    inverse_rms = []
    for distance in range(groups):
        total = jnp.sum(squares[distance * members : (distance + 1) * members], axis=0)
        if chips < LANES:
            total = jnp.concatenate(
                [total, jnp.zeros((LANES - chips, LANES), jnp.float32)], axis=0
            )
        inverse_rms.append(lax.rsqrt(total / D + 1e-05).T)
    gain = gain_ref[...]
    for shard in range(members):
        half = shard % 2
        scale = sum(
            inverse[half * rows : (half + 1) * rows, shard // 2 : shard // 2 + 1]
            * taken_of(shard, distance)
            for distance, inverse in enumerate(inverse_rms)
        )
        where = slice(shard * rows, (shard + 1) * rows)
        normed[where, :] = (hidden[where, :].astype(jnp.float32) * scale * gain).astype(normed.dtype)

    def drain(turn, carry):
        step, piece = turn // pieces, lax.rem(turn, pieces)

        @pl.when(step < chips - 1)
        def _():
            ring_copy(step, piece).wait_send()

        core_copy(step, piece).wait_send()
        return carry

    lax.fori_loop(0, chips * pieces, drain, 0)

    def drain_steps(step, carry):
        for distance in range(1, groups):
            peer_copy(step, distance).wait_send()
        return carry

    lax.fori_loop(0, chips, drain_steps, 0)

    def drain_squares(distance, carry):
        square_copy(distance).wait_send()
        return carry

    lax.fori_loop(1, groups * members, drain_squares, 0)


def local(groups, members, context, residual, out_weight, norm_gain, exit_layer, destination):
    rows, depth = context.shape
    group_rows, columns = residual.shape
    chips = members // 2
    pieces = max(1, min(4, rows // 16))
    anywhere = pl.BlockSpec(memory_space=pl.ANY)
    scalars = pl.BlockSpec(memory_space=pltpu.SMEM)
    out = jax.ShapeDtypeStruct((group_rows, columns), jnp.bfloat16)
    dma = pltpu.SemaphoreType.DMA
    return pl.pallas_call(
        functools.partial(kernel, groups, members, pieces),
        out_shape=(out, out),
        in_specs=[anywhere, anywhere, anywhere, pl.BlockSpec(memory_space=pltpu.VMEM), scalars, scalars],
        out_specs=(pl.BlockSpec(memory_space=pltpu.VMEM),) * 2,
        scratch_shapes=[
            pltpu.VMEM((chips, pieces, 2, rows, depth // pieces), jnp.bfloat16),
            pltpu.VMEM((pieces, depth // pieces, columns), jnp.bfloat16),
            pltpu.VMEM((group_rows, columns), jnp.bfloat16),
            pltpu.VMEM((2 * rows, columns), jnp.float32),
            pltpu.VMEM((chips, 2, rows, columns), jnp.bfloat16),
            pltpu.VMEM((groups - 1, chips, 2, rows, columns), jnp.bfloat16),
            pltpu.VMEM((groups * members, chips, LANES), jnp.float32),
            dma((chips, pieces)),
            dma((chips, pieces)),
            dma((chips, pieces)),
            dma((chips, pieces)),
            dma((pieces,)),
            dma((pieces,)),
            dma(()),
            dma((groups - 1, chips)),
            dma((groups - 1, chips)),
            dma((groups * members,)),
            dma((groups * members,)),
        ],
        compiler_params=pltpu.CompilerParams(
            collective_id=0, has_side_effects=True, vmem_limit_bytes=51 * 1024 * 1024
        ),
        cost_estimate=pl.CostEstimate(
            flops=2 * group_rows * depth * columns,
            bytes_accessed=2 * (rows * depth + depth * columns + 3 * group_rows * columns),
            transcendentals=0,
        ),
    )(context, residual, out_weight, norm_gain.reshape(1, columns), exit_layer, destination)


def solution(mesh):
    in_specs = (P(("dp", "fsdp"), None), P("dp", "fsdp"), P(None, "fsdp"), P("fsdp"), P(), P())
    out_specs = (P("dp", "fsdp"), P("dp", "fsdp"))
    body = functools.partial(local, mesh.shape["dp"], mesh.shape["fsdp"])
    return jax.shard_map(body, mesh=mesh, in_specs=in_specs, out_specs=out_specs, check_vma=False)
```

```python
import functools

import jax
import jax.numpy as jnp
from jax import lax
from jax.experimental import pallas as pl
from jax.experimental.pallas import tpu as pltpu
from jax.sharding import PartitionSpec as P

D = 8192
LAYER = 32
PLEN = 128
LANES = 128
MESH = pl.DeviceIdType.MESH


def kernel(
    groups, members, pieces,
    context_ref, residual_ref, weight_ref, gain_ref, exit_ref, dest_ref,
    hidden, normed,
    ctx, weight, residual, acc, stream, incoming, squares,
    ring_send, ring_recv, core_send, core_recv, own_sem, weight_sem, residual_sem,
    peer_send, peer_recv, square_send, square_recv,
):
    rows, depth = context_ref.shape
    width = depth // pieces
    passages = residual_ref.shape[0] // PLEN
    chips = members // 2
    group = lax.axis_index("dp")
    me = lax.axis_index("fsdp")
    core = lax.rem(me, 2)
    chip = me // 2

    def chip_at(place):
        return jnp.where(place < chips // 2, 2 * place, 2 * (chips - 1 - place) + 1)

    place = jnp.where(lax.rem(chip, 2) == 0, chip // 2, chips - 1 - chip // 2)
    ahead = lax.rem(place + jnp.where(core == 0, 1, chips - 1), chips)
    target = chip_at(ahead) * 2 + core
    sibling = chip * 2 + 1 - core

    def shard_of(step, half):
        shift = chips - step if half == 0 else step
        return chip_at(lax.rem(place + shift, chips)) * 2 + half

    def ring_copy(step, piece, source=None):
        return pltpu.make_async_remote_copy(
            src_ref=ctx.at[step, piece, core] if source is None else source,
            dst_ref=ctx.at[step + 1, piece, core],
            send_sem=ring_send.at[step, piece],
            recv_sem=ring_recv.at[step + 1, piece],
            device_id=(group, target),
            device_id_type=MESH,
        )

    def core_copy(step, piece, source=None):
        return pltpu.make_async_remote_copy(
            src_ref=ctx.at[step, piece, core] if source is None else source,
            dst_ref=ctx.at[step, piece, core],
            send_sem=core_send.at[step, piece],
            recv_sem=core_recv.at[step, piece],
            device_id=(group, sibling),
            device_id_type=MESH,
        )

    def own_piece(piece):
        return context_ref.at[:, pl.ds(piece * width, width)]

    def own_copy(piece):
        return pltpu.make_async_copy(own_piece(piece), ctx.at[0, piece, core], own_sem.at[piece])

    def weight_copy(piece):
        return pltpu.make_async_copy(
            weight_ref.at[pl.ds(piece * width, width), :], weight.at[piece], weight_sem.at[piece]
        )

    residual_copy = pltpu.make_async_copy(residual_ref, residual, residual_sem)

    def peer_copy(step, distance):
        return pltpu.make_async_remote_copy(
            src_ref=stream.at[step],
            dst_ref=incoming.at[distance - 1, step],
            send_sem=peer_send.at[distance - 1, step],
            recv_sem=peer_recv.at[distance - 1, step],
            device_id=(lax.rem(group + distance, groups), me),
            device_id_type=MESH,
        )

    def square_copy(index):
        return pltpu.make_async_remote_copy(
            src_ref=squares.at[0],
            dst_ref=squares.at[index],
            send_sem=square_send.at[index],
            recv_sem=square_recv.at[index],
            device_id=(
                lax.rem(group + index // members, groups),
                lax.rem(me + lax.rem(index, members), members),
            ),
            device_id_type=MESH,
        )

    def taken_of(shard, distance):
        where = lax.rem(group + groups - distance, groups) * passages + shard * rows // PLEN
        taken = jnp.logical_and(exit_ref[where] > LAYER, dest_ref[where] == group)
        return taken.astype(jnp.int32).astype(jnp.float32)

    def rows_of(shard):
        return pl.ds(pl.multiple_of(shard * rows, rows), rows)

    for piece in range(pieces):
        own_copy(piece).start()
    for piece in range(pieces):
        weight_copy(piece).start()
    residual_copy.start()
    squares[0] = jnp.zeros(squares.shape[1:], jnp.float32)

    barrier = pltpu.get_barrier_semaphore()

    behind = lax.rem(place + jnp.where(core == 0, chips - 1, 1), chips)
    for member in (target, chip_at(behind) * 2 + core, sibling):
        pl.semaphore_signal(barrier, inc=1, device_id=(group, member), device_id_type=MESH)
    for distance in range(1, groups):
        pl.semaphore_signal(
            barrier, inc=1, device_id=(lax.rem(group + distance, groups), me), device_id_type=MESH
        )
    pl.semaphore_wait(barrier, 3 + groups - 1)

    for piece in range(pieces):
        ring_copy(0, piece, own_piece(piece)).start()
    for piece in range(pieces):
        core_copy(0, piece, own_piece(piece)).start()

    def add_squares(step, blocks):
        halves = []
        for block in blocks:
            square = block * block
            parts = [square[:, at : at + LANES] for at in range(0, square.shape[1], LANES)]
            halves.append(functools.reduce(jnp.add, parts))
        if 2 * rows < LANES:
            halves.append(jnp.zeros((LANES - 2 * rows, LANES), jnp.float32))
        sums = jnp.sum(jnp.concatenate(halves, axis=0).T, axis=0, keepdims=True)
        lane = lax.broadcasted_iota(jnp.int32, sums.shape, 1)
        for half in range(2):
            own = jnp.logical_and(lane >= half * rows, lane < (half + 1) * rows)
            squares[0, pl.ds(shard_of(step, half) // 2, 1), :] += jnp.where(own, sums, 0.0)

    def finish(step):
        for distance in range(1, groups):
            peer_copy(step, distance).wait_recv()
        for half in range(2):
            shard = shard_of(step, half)
            chosen = None
            for distance in range(groups):
                block = stream[step, half] if distance == 0 else incoming[distance - 1, step, half]
                term = block.astype(jnp.float32) * taken_of(shard, distance)
                chosen = term if chosen is None else chosen + term
            hidden[rows_of(shard), :] = chosen.astype(hidden.dtype)

    def body(turn, carry):
        @pl.when(jnp.logical_and(turn >= pieces, turn < chips * pieces))
        def _():
            step, piece = turn // pieces, lax.rem(turn, pieces)
            ring_copy(step - 1, piece).wait_recv()

            @pl.when(step < chips - 1)
            def _():
                ring_copy(step, piece).start()

            core_copy(step, piece).start()

        @pl.when(turn >= 1)
        def _():
            step, piece = (turn - 1) // pieces, lax.rem(turn - 1, pieces)

            @pl.when(step == 0)
            def _():
                own_copy(piece).wait()
                weight_copy(piece).wait()

            core_copy(step, piece).wait_recv()
            product = jnp.dot(
                ctx[step, piece].reshape(2 * rows, width),
                weight[piece],
                preferred_element_type=jnp.float32,
            )

            @pl.when(piece == 0)
            def _():
                acc[...] = product

            @pl.when(piece > 0)
            def _():
                acc[...] += product

            @pl.when(piece == pieces - 1)
            def _():
                @pl.when(step == 0)
                def _():
                    residual_copy.wait()

                blocks = []
                for half in range(2):
                    before = residual[rows_of(shard_of(step, half)), :].astype(jnp.float32)
                    block = (acc[half * rows : (half + 1) * rows, :] + before).astype(stream.dtype)
                    stream[step, half] = block
                    blocks.append(block.astype(jnp.float32))
                for distance in range(1, groups):
                    peer_copy(step, distance).start()

                add_squares(step, blocks)

                @pl.when(jnp.logical_and(step > 0, step < chips - 1))
                def _():
                    finish(step - 1)

        return carry

    lax.fori_loop(0, chips * pieces + 1, body, 0)

    def send_squares(index, carry):
        square_copy(groups * members - index).start()
        return carry

    def take_squares(index, carry):
        square_copy(index).wait_recv()
        return carry

    lax.fori_loop(1, groups * members, send_squares, 0)
    finish(chips - 2)
    finish(chips - 1)
    lax.fori_loop(1, groups * members, take_squares, 0)
    inverse_rms = []
    for distance in range(groups):
        total = jnp.sum(squares[distance * members : (distance + 1) * members], axis=0)
        if chips < LANES:
            total = jnp.concatenate(
                [total, jnp.zeros((LANES - chips, LANES), jnp.float32)], axis=0
            )
        inverse_rms.append(lax.rsqrt(total / D + 1e-05).T)
    gain = gain_ref[...]
    for shard in range(members):
        half = shard % 2
        scale = sum(
            inverse[half * rows : (half + 1) * rows, shard // 2 : shard // 2 + 1]
            * taken_of(shard, distance)
            for distance, inverse in enumerate(inverse_rms)
        )
        where = slice(shard * rows, (shard + 1) * rows)
        normed[where, :] = (hidden[where, :].astype(jnp.float32) * scale * gain).astype(normed.dtype)

    def drain(turn, carry):
        step, piece = turn // pieces, lax.rem(turn, pieces)

        @pl.when(step < chips - 1)
        def _():
            ring_copy(step, piece).wait_send()

        core_copy(step, piece).wait_send()
        return carry

    lax.fori_loop(0, chips * pieces, drain, 0)

    def drain_steps(step, carry):
        for distance in range(1, groups):
            peer_copy(step, distance).wait_send()
        return carry

    lax.fori_loop(0, chips, drain_steps, 0)

    def drain_squares(distance, carry):
        square_copy(distance).wait_send()
        return carry

    lax.fori_loop(1, groups * members, drain_squares, 0)


def local(groups, members, context, residual, out_weight, norm_gain, exit_layer, destination):
    rows, depth = context.shape
    group_rows, columns = residual.shape
    chips = members // 2
    pieces = max(1, min(4, rows // 16))
    anywhere = pl.BlockSpec(memory_space=pl.ANY)
    scalars = pl.BlockSpec(memory_space=pltpu.SMEM)
    out = jax.ShapeDtypeStruct((group_rows, columns), jnp.bfloat16)
    dma = pltpu.SemaphoreType.DMA
    return pl.pallas_call(
        functools.partial(kernel, groups, members, pieces),
        out_shape=(out, out),
        in_specs=[anywhere, anywhere, anywhere, pl.BlockSpec(memory_space=pltpu.VMEM), scalars, scalars],
        out_specs=(pl.BlockSpec(memory_space=pltpu.VMEM),) * 2,
        scratch_shapes=[
            pltpu.VMEM((chips, pieces, 2, rows, depth // pieces), jnp.bfloat16),
            pltpu.VMEM((pieces, depth // pieces, columns), jnp.bfloat16),
            pltpu.VMEM((group_rows, columns), jnp.bfloat16),
            pltpu.VMEM((2 * rows, columns), jnp.float32),
            pltpu.VMEM((chips, 2, rows, columns), jnp.bfloat16),
            pltpu.VMEM((groups - 1, chips, 2, rows, columns), jnp.bfloat16),
            pltpu.VMEM((groups * members, chips, LANES), jnp.float32),
            dma((chips, pieces)),
            dma((chips, pieces)),
            dma((chips, pieces)),
            dma((chips, pieces)),
            dma((pieces,)),
            dma((pieces,)),
            dma(()),
            dma((groups - 1, chips)),
            dma((groups - 1, chips)),
            dma((groups * members,)),
            dma((groups * members,)),
        ],
        compiler_params=pltpu.CompilerParams(
            collective_id=0, has_side_effects=True, vmem_limit_bytes=51 * 1024 * 1024
        ),
        cost_estimate=pl.CostEstimate(
            flops=2 * group_rows * depth * columns,
            bytes_accessed=2 * (rows * depth + depth * columns + 3 * group_rows * columns),
            transcendentals=0,
        ),
    )(context, residual, out_weight, norm_gain.reshape(1, columns), exit_layer, destination)


def solution(mesh):
    in_specs = (P(("dp", "fsdp"), None), P("dp", "fsdp"), P(None, "fsdp"), P("fsdp"), P(), P())
    out_specs = (P("dp", "fsdp"), P("dp", "fsdp"))
    body = functools.partial(local, mesh.shape["dp"], mesh.shape["fsdp"])
    return jax.shard_map(body, mesh=mesh, in_specs=in_specs, out_specs=out_specs, check_vma=False)
```
